512 devices in a mesh: pipe: 16 (over x, z_hi, core), expert: 32 (over z_lo, y).
Axes of the slice: x: 4, y: 8, z: 8 (z_hi: 2, z_lo: 4; z = z_hi * 4 + z_lo), core: 2. Of those that a mesh axis runs over, the one named last changes fastest.
Arguments:
- fwd_in: bfloat16 [32768, 3584], P(('pipe', 'expert')), may hold values from -6 to 6
- fwd_routes: int32 [32768, 2], P(('pipe', 'expert')), may hold values from 0 to 3, all different within a row; in each aligned block of 64 rows (0 to 63, 64 to 127, ...) at most 34 rows name the same one
- router: bfloat16 [16, 3584, 4], P('pipe'), may hold values from -0.09375 to 0.09375
- bwd_in: bfloat16 [32768, 3584], P(('pipe', 'expert')), may hold values from -6 to 6
- bwd_routes: int32 [32768, 2], P(('pipe', 'expert')), may hold values from 0 to 3, all different within a row; in each aligned block of 64 rows (0 to 63, 64 to 127, ...) at most 34 rows name the same one
- bwd_gates: float32 [32768, 2], P(('pipe', 'expert')), may hold values from 0.1 to 0.9
- w_gate: bfloat16 [16, 3584, 4096], P('pipe', None, 'expert'), may hold values from -0.09375 to 0.09375
- w_up: bfloat16 [16, 3584, 4096], P('pipe', None, 'expert'), may hold values from -0.09375 to 0.09375
- w_down: bfloat16 [16, 4096, 3584], P('pipe', 'expert'), may hold values from -0.1875 to 0.1875
- saved_pre: bfloat16 [2, 16, 1088, 4096], P(None, 'pipe', None, 'expert'), may hold values from -5 to 5
Outputs:
- fwd_out: bfloat16 [32768, 3584], P(('pipe', 'expert'))
- bwd_out: bfloat16 [32768, 3584], P(('pipe', 'expert'))
The draws below stay inside these ranges and needn't reach their ends.
Inputs may be any that keep to these rules, and one draw needn't show every extreme that they name: `fwd_routes`: in each device's 64 tokens (aligned blocks) no expert is named by more than 34 pairs, a bound that some block reaches; a token's experts differ. `bwd_routes`: as for fwd_routes.
All inputs are finite; a program needn't handle non-finite values.
Results may differ from the reference program's by a relative error of at most 0.0054.
Values may be sent and summed in bfloat16 or wider, within the bound.
No kernel may reach another device: no remote copies, remote signals or barrier semaphores. Data moves between devices by JAX's collectives and lax.ppermute only.
A program may use at most 128 MiB of HBM per device.

```python
import math
import jax
import jax.numpy as jnp
import numpy as np
from jax import lax

D = 3584
FFE = 1024
EXPERTS = 4
TOP = 2
TOK_DEV = 64
CAP = 34
TOKENS = 32768
N_PIPE = 16
N_EXPERT = 32


def steps_of(key, dims, split, low, top_value):
    def one(dim, blocks):
        steps = jax.random.uniform(jax.random.fold_in(jax.random.fold_in(key, 6), dim), (blocks,), jnp.float32, low / len(split), top_value / len(split))
        return jnp.repeat(jnp.exp(steps), dims[dim] // blocks).reshape((-1,) + (1,) * (len(dims) - dim - 1))

    loudness = one(*split[0])
    for cut in split[1:]:
        loudness = loudness * one(*cut)
    return loudness


def routed_block(rng, own, number, rows, number_of, top, bound, lean):
    sequence = jax.random.permutation(rng, number_of)
    heavy_load, usual = load_shares(number_of, rows * top, bound, lean, True), load_shares(number_of, rows * top, bound, lean, False)
    places = jnp.arange(number_of)

    def named(sizes, offset_by):
        used = int((sizes > 0).sum())
        fixed = max(1, used // 4)
        passed = fixed + (places - fixed + offset_by * (used - fixed)) % max(1, number_of - fixed)
        return jnp.zeros((number_of,), jnp.int32).at[sequence[jnp.where(places < fixed, places, passed)]].set(jnp.asarray(sizes, jnp.int32))

    sizes = jnp.where(number % 4 == 0, named(heavy_load, number // 4), named(usual, number - number // 4 - 1))
    mixed = jax.random.permutation(jax.random.fold_in(own, 3), number_of)
    donor, receiver = mixed[0:number_of // 2 * 2:2], mixed[1:number_of // 2 * 2:2]
    room = jnp.minimum(sizes[donor] - 1, bound - sizes[receiver]) // 2
    room = jnp.where((donor == sequence[0]) | (receiver == sequence[0]) | (sizes[receiver] == 0), 0, jnp.maximum(room, 0))
    passed = jax.random.randint(jax.random.fold_in(own, 4), (number_of // 2,), 0, 1 << 20) % (room + 1)
    sizes = sizes.at[donor].add(-passed).at[receiver].add(passed)
    labels = jnp.searchsorted(jnp.cumsum(sizes), jnp.arange(rows * top), side="right").astype(jnp.int32)
    grid = labels.reshape(top, rows).T
    grid = grid[jax.random.permutation(jax.random.fold_in(own, 1), rows)]
    offset_by = jax.random.randint(jax.random.fold_in(own, 2), (rows, 1), 0, top)
    return jnp.take_along_axis(grid, (jnp.arange(top)[None, :] + offset_by) % top, axis=1)


def load_shares(count, total, limit, slope, full):
    loads = [(1 << 20) // math.isqrt(standing ** slope) + 1 for standing in range(1, count + 1)]
    largest = limit if full else min(limit, max(-(-total // count), total * loads[0] // sum(loads)))
    least = 1 if total - largest >= count - 1 else 0
    holding, rest = [largest] + [least] * (count - 1), total - largest - least * (count - 1)
    while rest > 0:
        movable = [i for i in range(1, count) if holding[i] < largest] or [i for i in range(1, count) if holding[i] < limit]
        whole, left = sum([loads[i] for i in movable]), rest
        for i in movable:
            addition = min(limit - holding[i], max(1, left * loads[i] // whole), rest)
            holding[i] = holding[i] + addition
            rest = rest - addition
    return np.array(holding)


def gaussian(key, extent, scale, limit, shards=(), kind=jnp.bfloat16):
    drawn = scale * jax.random.normal(key, extent, jnp.float32)
    if shards:
        drawn = drawn * steps_of(key, extent, shards, -0.22, 0.18)
    return jnp.clip(drawn, -limit, limit).astype(kind)


def setup_inputs(seed: int = 0) -> dict:
    seeds = jax.random.split(jax.random.key(seed), 11)
    fwd_in = gaussian(seeds[0], (TOKENS, D), 1.0, 6.0, ((0, 512),))
    fwd_routes_keys = jax.random.split(jax.random.fold_in(seeds[1], 1), TOKENS // TOK_DEV)
    fwd_routes_turns = jax.random.permutation(jax.random.fold_in(seeds[1], 3), TOKENS // TOK_DEV)
    fwd_routes = jax.vmap(lambda own, number: routed_block(jax.random.fold_in(seeds[1], 2), own, number, TOK_DEV, EXPERTS, TOP, CAP, 2))(fwd_routes_keys, fwd_routes_turns).reshape((TOKENS, TOP))
    router = gaussian(seeds[2], (N_PIPE, D, EXPERTS), D ** -0.5, 0.09375, ((0, 16),))
    bwd_in = gaussian(seeds[3], (TOKENS, D), 1.0, 6.0, ((0, 512),))
    bwd_routes_keys = jax.random.split(jax.random.fold_in(seeds[4], 1), TOKENS // TOK_DEV)
    bwd_routes_turns = jax.random.permutation(jax.random.fold_in(seeds[4], 3), TOKENS // TOK_DEV)
    bwd_routes = jax.vmap(lambda own, number: routed_block(jax.random.fold_in(seeds[4], 2), own, number, TOK_DEV, EXPERTS, TOP, CAP, 2))(bwd_routes_keys, bwd_routes_turns).reshape((TOKENS, TOP))
    bwd_gates = jnp.clip(0.1 + 0.79999997 * jax.random.uniform(seeds[5], (TOKENS, TOP), jnp.float32) ** steps_of(seeds[5], (TOKENS, TOP), ((0, 512),), -0.2, 0.2), 0.1, 0.9)
    w_gate = gaussian(seeds[6], (N_PIPE, D, EXPERTS * FFE), D ** -0.5, 0.09375, ((0, 16), (2, 32)))
    w_up = gaussian(seeds[7], (N_PIPE, D, EXPERTS * FFE), D ** -0.5, 0.09375, ((0, 16), (2, 32)))
    w_down = gaussian(seeds[8], (N_PIPE, EXPERTS * FFE, D), FFE ** -0.5, 0.1875, ((0, 16), (1, 32)))
    saved_pre = gaussian(seeds[9], (2, N_PIPE, N_EXPERT * CAP, EXPERTS * FFE), 1.0, 5.0, ((1, 16), (3, 32)))
    return {"fwd_in": fwd_in, "fwd_routes": fwd_routes, "router": router, "bwd_in": bwd_in, "bwd_routes": bwd_routes, "bwd_gates": bwd_gates, "w_gate": w_gate, "w_up": w_up, "w_down": w_down, "saved_pre": saved_pre}


def slot_places(routes):
    rows = routes.shape[0]
    onehot = (routes[:, :, None] == jnp.arange(EXPERTS, dtype=jnp.int32)[None, None, :]).astype(jnp.int32)
    onehot = onehot.reshape(rows * TOP, EXPERTS)
    before = jnp.cumsum(onehot, axis=0) - onehot
    slot = jnp.sum(before * onehot, axis=1).reshape(rows, TOP)
    return (routes * CAP + slot).astype(jnp.int32)


def gather_rows(places, data):
    spots = jnp.arange(EXPERTS * CAP, dtype=jnp.int32)
    select = jnp.sum((places[None, :, :] == spots[:, None, None]).astype(jnp.float32), axis=2)
    return jnp.dot(select.astype(jnp.bfloat16), data, preferred_element_type=jnp.float32).astype(jnp.bfloat16)


def spread_back(places, weights, values):
    spots = jnp.arange(EXPERTS * CAP, dtype=jnp.int32)
    combine = jnp.sum(jnp.where(places[:, :, None] == spots[None, None, :], weights[:, :, None], 0.0), axis=1)
    return jnp.dot(combine, values, precision=lax.Precision.HIGHEST)


def lane_tree(terms):
    while terms.shape[0] > 1:
        half = terms.shape[0] // 2
        terms = lax.optimization_barrier((terms[:half].astype(jnp.float32) + terms[half:].astype(jnp.float32)).astype(jnp.bfloat16))
    return terms[0].astype(jnp.float32)


def reference(fwd_in, fwd_routes, router, bwd_in, bwd_routes, bwd_gates, w_gate, w_up, w_down, saved_pre):
    lanes = N_EXPERT // EXPERTS
    share = FFE // lanes
    fwd_stack = fwd_in.reshape(N_PIPE, N_EXPERT, TOK_DEV, D)
    bwd_stack = bwd_in.reshape(N_PIPE, N_EXPERT, TOK_DEV, D)
    froutes = fwd_routes.reshape(N_PIPE, N_EXPERT, TOK_DEV, TOP)
    broutes = bwd_routes.reshape(N_PIPE, N_EXPERT, TOK_DEV, TOP)
    bgates = bwd_gates.reshape(N_PIPE, N_EXPERT, TOK_DEV, TOP)

    def section(p):
        inputs = fwd_stack[(p + N_PIPE - 1) % N_PIPE]
        cotan = bwd_stack[(p + 1) % N_PIPE]
        fplaces = jax.vmap(slot_places)(froutes[p])
        bplaces = jax.vmap(slot_places)(broutes[p])
        xbuf = jax.vmap(gather_rows)(fplaces, inputs).reshape(N_EXPERT, EXPERTS, CAP, D)
        dbuf = jax.vmap(gather_rows)(bplaces, cotan).reshape(N_EXPERT, EXPERTS, CAP, D)
        logits = jnp.dot(inputs.reshape(N_EXPERT * TOK_DEV, D), router[p], preferred_element_type=jnp.float32)
        score = jax.nn.sigmoid(logits)
        chosen = jnp.take_along_axis(score, froutes[p].reshape(N_EXPERT * TOK_DEV, TOP), axis=1)
        gates = (chosen / jnp.sum(chosen, axis=1, keepdims=True)).reshape(N_EXPERT, TOK_DEV, TOP)
        wg_all = w_gate[p]
        wu_all = w_up[p]
        wd_all = w_down[p]
        outs_f = []
        outs_b = []
        for e in range(EXPERTS):
            wg = wg_all[:, e * FFE:(e + 1) * FFE]
            wu = wu_all[:, e * FFE:(e + 1) * FFE]
            wd = wd_all[e * FFE:(e + 1) * FFE, :]
            rows = xbuf[:, e].reshape(N_EXPERT * CAP, D)
            gpre = jnp.dot(rows, wg, preferred_element_type=jnp.float32)
            upre = jnp.dot(rows, wu, preferred_element_type=jnp.float32)
            hidden = (jax.nn.silu(gpre) * upre).astype(jnp.bfloat16)
            parts = jnp.einsum("rgf,gfd->grd", hidden.astype(jnp.float32).reshape(N_EXPERT * CAP, lanes, share),
                               wd.astype(jnp.float32).reshape(lanes, share, D))
            outs_f.append(lane_tree(parts.astype(jnp.bfloat16)).reshape(N_EXPERT, CAP, D))
            grads = dbuf[:, e].reshape(N_EXPERT * CAP, D)
            apre = saved_pre[0, p][:, e * FFE:(e + 1) * FFE].astype(jnp.float32)
            bpre = saved_pre[1, p][:, e * FFE:(e + 1) * FFE].astype(jnp.float32)
            dhid = jnp.dot(grads, wd.T, preferred_element_type=jnp.float32)
            sig = jax.nn.sigmoid(apre)
            dgate = (dhid * bpre * sig * (1.0 + apre * (1.0 - sig))).astype(jnp.bfloat16)
            dup = (dhid * apre * sig).astype(jnp.bfloat16)
            bparts = jnp.einsum("rgf,dgf->grd", dgate.astype(jnp.float32).reshape(N_EXPERT * CAP, lanes, share),
                                wg.astype(jnp.float32).reshape(D, lanes, share))
            bparts = bparts + jnp.einsum("rgf,dgf->grd", dup.astype(jnp.float32).reshape(N_EXPERT * CAP, lanes, share),
                                         wu.astype(jnp.float32).reshape(D, lanes, share))
            outs_b.append(lane_tree(bparts.astype(jnp.bfloat16)).reshape(N_EXPERT, CAP, D))
        ybuf = jnp.stack(outs_f, axis=1).reshape(N_EXPERT, EXPERTS * CAP, D)
        zbuf = jnp.stack(outs_b, axis=1).reshape(N_EXPERT, EXPERTS * CAP, D)
        fwd = inputs.astype(jnp.float32) + jax.vmap(spread_back)(fplaces, gates, ybuf)
        bwd = cotan.astype(jnp.float32) + jax.vmap(spread_back)(bplaces, bgates[p], zbuf)
        return fwd.astype(jnp.bfloat16), bwd.astype(jnp.bfloat16)

    fwd_all, bwd_all = lax.map(section, jnp.arange(N_PIPE, dtype=jnp.int32))
    return fwd_all.reshape(TOKENS, D), bwd_all.reshape(TOKENS, D)
```

```python
import jax
import jax.numpy as jnp
from jax import lax
from jax.sharding import Mesh, PartitionSpec as P

EXPERTS = 4
TOP = 2
CAP = 34
LANES = 8
INFO = 128

AXES = ("x", "h", "c", "u", "v", "y")
SIZES = (4, 2, 2, 2, 2, 8)


def swap(array):
    return lax.ppermute(array, ("c", "u"), [(0, 0), (1, 2), (2, 1), (3, 3)])


def shift_and_swap(array, by):
    pairs = []
    for p in range(16):
        q = (p + by) % 16
        for u in range(2):
            source = p * 2 + u
            target = (q // 2) * 4 + u * 2 + q % 2
            pairs.append((source, target))
    return lax.ppermute(array, ("x", "h", "c", "u"), pairs)


def other_plane(array):
    return lax.ppermute(array, "v", [(0, 1), (1, 0)])


def other_core(array):
    return lax.ppermute(array, "c", [(0, 1), (1, 0)])


def experts_of_lane(block):
    own = swap(block)
    near = other_plane(own)
    return (own, near, other_core(own), other_core(near))


def saved_of_lane(saved, number):
    rows = saved.shape[1] // EXPERTS
    expert = lax.axis_index("u") * 2 + lax.axis_index("v")
    part = lax.dynamic_slice_in_dim(saved, (expert ^ number) * rows, rows, axis=1)
    pairs = []
    for c in range(2):
        for e in range(4):
            z = e ^ number
            pairs.append((c * 4 + e, (z // 2) * 4 + c * 2 + z % 2))
    return lax.ppermute(part, ("c", "u", "v"), pairs)


def slot_places(routes):
    rows = routes.shape[0]
    onehot = (routes[:, :, None] == jnp.arange(EXPERTS, dtype=jnp.int32)[None, None, :]).astype(
        jnp.int32
    )
    onehot = onehot.reshape(rows * TOP, EXPERTS)
    before = jnp.cumsum(onehot, axis=0) - onehot
    slot = jnp.sum(before * onehot, axis=1).reshape(rows, TOP)
    return routes * CAP + slot


def three_terms(values):
    high = lax.reduce_precision(values, 8, 7)
    middle = lax.reduce_precision(values - high, 8, 7)
    low = values - high - middle
    return [high, middle, low]


def body(
    fwd_in, fwd_routes, router, bwd_in, bwd_routes, bwd_gates, w_gate, w_up, w_down, saved_pre
):
    width = fwd_in.shape[1]
    tokens = fwd_in.shape[0]
    x = shift_and_swap(fwd_in, 1)
    q = shift_and_swap(bwd_in, -1)
    info = jnp.concatenate(
        [fwd_routes.astype(jnp.float32), slot_places(bwd_routes).astype(jnp.float32)]
        + three_terms(bwd_gates),
        axis=1,
    ).astype(jnp.bfloat16)
    info = swap(jnp.pad(info, ((0, 0), (0, INFO - info.shape[1]))))
    columns = swap(router[0].T)
    wgu = experts_of_lane(jnp.concatenate([w_gate[0], w_up[0]], axis=1))
    wd = experts_of_lane(w_down[0])
    saved = [saved_of_lane(saved_pre[:, 0], number) for number in range(EXPERTS)]

    gathered = lax.all_gather(jnp.concatenate([x, info], axis=1), "y", axis=0, tiled=True)
    grads = lax.all_gather(q, "y", axis=0, tiled=True)
    rows = gathered[:, :width]
    facts = gathered[:, width:].astype(jnp.float32)
    froutes = facts[:, 0:2].astype(jnp.int32)
    bplaces = facts[:, 2:4].astype(jnp.int32)
    bgates = facts[:, 4:6] + facts[:, 6:8] + facts[:, 8:10]
    broutes = bplaces // CAP
    e0 = lax.axis_index("c") * 2 + lax.axis_index("v")

    score = jax.nn.sigmoid(
        lax.dot_general(rows, columns, (((1,), (1,)), ((), ())), preferred_element_type=jnp.float32)
    )
    chosen = jnp.take_along_axis(score, froutes, axis=1)
    fgates = chosen / jnp.sum(chosen, axis=1, keepdims=True)

    source = jnp.arange(rows.shape[0], dtype=jnp.int32)[:, None] // tokens
    hidden = []
    for number in range(EXPERTS):
        named = froutes == (e0 ^ number)
        weight = jnp.sum(jnp.where(named, fgates, 0.0), axis=1, keepdims=True)
        pre = jnp.dot(rows, wgu[number], preferred_element_type=jnp.float32)
        half = pre.shape[1] // 2
        hidden.append((jax.nn.silu(pre[:, :half]) * pre[:, half:] * weight).astype(jnp.bfloat16))
    fpart = jnp.dot(
        jnp.concatenate(hidden, axis=1),
        jnp.concatenate(wd, axis=0),
        preferred_element_type=jnp.float32,
    ).astype(jnp.bfloat16)
    fsum = lax.psum_scatter(fpart, "y", scatter_dimension=0, tiled=True)

    dpre = []
    for number in range(EXPERTS):
        named = broutes == (e0 ^ number)
        weight = jnp.sum(jnp.where(named, bgates, 0.0), axis=1, keepdims=True)
        slot = source * CAP + bplaces - broutes * CAP + 1
        spot = jnp.sum(jnp.where(named, slot, 0), axis=1, keepdims=True) - 1
        pick = (spot == jnp.arange(LANES * CAP, dtype=jnp.int32)[None, :]).astype(jnp.bfloat16)
        apre = jnp.dot(pick, saved[number][0], preferred_element_type=jnp.float32)
        bpre = jnp.dot(pick, saved[number][1], preferred_element_type=jnp.float32)
        dhid = lax.dot_general(
            grads, wd[number], (((1,), (1,)), ((), ())), preferred_element_type=jnp.float32
        )
        sig = jax.nn.sigmoid(apre)
        dhid = dhid * weight
        dpre.append((dhid * bpre * sig * (1.0 + apre * (1.0 - sig))).astype(jnp.bfloat16))
        dpre.append((dhid * apre * sig).astype(jnp.bfloat16))
    bpart = lax.dot_general(
        jnp.concatenate(dpre, axis=1),
        jnp.concatenate(wgu, axis=1),
        (((1,), (1,)), ((), ())),
        preferred_element_type=jnp.float32,
    ).astype(jnp.bfloat16)
    bsum = lax.psum_scatter(bpart, "y", scatter_dimension=0, tiled=True)

    fwd_out = (x.astype(jnp.float32) + fsum.astype(jnp.float32)).astype(jnp.bfloat16)
    bwd_out = (q.astype(jnp.float32) + bsum.astype(jnp.float32)).astype(jnp.bfloat16)
    return (swap(fwd_out), swap(bwd_out))


def solution(mesh):
    fine = Mesh(mesh.devices.reshape(SIZES), AXES)
    section = ("x", "h", "c")
    part = ("u", "v", "y")
    both = P(AXES, None)
    in_specs = (
        both,
        both,
        P(section, None, None),
        both,
        both,
        both,
        P(section, None, part),
        P(section, None, part),
        P(section, part, None),
        P(None, section, None, part),
    )
    return jax.shard_map(
        body, mesh=fine, in_specs=in_specs, out_specs=(both, both), check_vma=False
    )
```

```python
import jax
import jax.numpy as jnp
from jax import lax
from jax.experimental import pallas as pl
from jax.experimental.pallas import tpu as pltpu
from jax.sharding import Mesh, PartitionSpec as P

EXPERTS = 4
TOP = 2
CAP = 34
LANES = 8
INFO = 128
VMEM = 32 << 20

AXES = ("x", "h", "c", "u", "v", "y")
SIZES = (4, 2, 2, 2, 2, 8)


def swap(array):
    return lax.ppermute(array, ("c", "u"), [(0, 0), (1, 2), (2, 1), (3, 3)])


def shift_and_swap(array, by):
    pairs = []
    for p in range(16):
        q = (p + by) % 16
        for u in range(2):
            source = p * 2 + u
            target = (q // 2) * 4 + u * 2 + q % 2
            pairs.append((source, target))
    return lax.ppermute(array, ("x", "h", "c", "u"), pairs)


def other_plane(array):
    return lax.ppermute(array, "v", [(0, 1), (1, 0)])


def other_core(array):
    return lax.ppermute(array, "c", [(0, 1), (1, 0)])


def saved_of_lane(saved, number):
    rows = saved.shape[1] // EXPERTS
    expert = lax.axis_index("u") * 2 + lax.axis_index("v")
    part = lax.dynamic_slice_in_dim(saved, (expert ^ number) * rows, rows, axis=1)
    pairs = []
    for c in range(2):
        for e in range(4):
            z = e ^ number
            pairs.append((c * 4 + e, (z // 2) * 4 + c * 2 + z % 2))
    return lax.ppermute(jnp.concatenate([part[0], part[1]], axis=1), ("c", "u", "v"), pairs)


def slot_places(routes):
    rows = routes.shape[0]
    onehot = (routes[:, :, None] == jnp.arange(EXPERTS, dtype=jnp.int32)[None, None, :]).astype(
        jnp.int32
    )
    onehot = onehot.reshape(rows * TOP, EXPERTS)
    before = jnp.cumsum(onehot, axis=0) - onehot
    slot = jnp.sum(before * onehot, axis=1).reshape(rows, TOP)
    return routes * CAP + slot


def three_terms(values):
    high = lax.reduce_precision(values, 8, 7)
    middle = lax.reduce_precision(values - high, 8, 7)
    low = values - high - middle
    return [high, middle, low]


def neighbour(array, by):
    return lax.ppermute(array, "y", [(i, (i + by) % LANES) for i in range(LANES)])


def own_block(terms, distance):
    rows = terms.shape[0] // LANES
    place = (lax.axis_index("y") + distance) % LANES
    return lax.dynamic_slice_in_dim(terms, place * rows, rows, axis=0)


class Chain:
    def __init__(self, terms, by, length):
        self.terms, self.by, self.left = terms, by, length
        self.total = own_block(terms, by * length)

    def step(self):
        if self.left:
            self.left -= 1
            received = neighbour(self.total.astype(jnp.bfloat16), self.by).astype(jnp.float32)
            self.total = received
            if self.left:
                self.total = received + own_block(self.terms, self.by * self.left)


def slopes_kernel(e0_ref, info_ref, *refs):
    saved_refs = refs[0:4]
    slope_gate_ref, slope_up_ref = refs[4:]
    count = info_ref.shape[0]
    slots, lane = saved_refs[0].shape[0], saved_refs[0].shape[1] // 2
    facts = info_ref[...].astype(jnp.float32)
    places = [facts[:, 2:3], facts[:, 3:4]]
    gates = [
        facts[:, 4 + k : 5 + k] + facts[:, 6 + k : 7 + k] + facts[:, 8 + k : 9 + k]
        for k in range(TOP)
    ]
    source = lax.broadcasted_iota(jnp.int32, (count, 1), 0) // (count // LANES)
    start = (source * CAP + 1).astype(jnp.float32)
    spot = (lax.broadcasted_iota(jnp.int32, (1, slots), 1) + 1).astype(jnp.float32)
    for block in range(EXPERTS):
        low = ((e0_ref[0] ^ block) * CAP).astype(jnp.float32)
        weight = jnp.zeros((count, 1), jnp.float32)
        target = jnp.zeros((count, 1), jnp.float32)
        for k in range(TOP):
            named = jnp.logical_and(places[k] >= low, places[k] < low + CAP)
            weight = weight + jnp.where(named, gates[k], 0.0)
            target = target + jnp.where(named, start + places[k] - low, 0.0)
        pick = jnp.where(target == spot, 1.0, 0.0).astype(jnp.bfloat16)
        kept = jnp.dot(pick, saved_refs[block][...], preferred_element_type=jnp.float32)
        apre, bpre = kept[:, :lane], kept[:, lane:]
        sig = jax.nn.sigmoid(apre)
        columns = slice(block * lane, (block + 1) * lane)
        slope_gate_ref[:, columns] = bpre * sig * (1.0 + apre * (1.0 - sig)) * weight
        slope_up_ref[:, columns] = apre * sig * weight


def slopes(e0, gathered, width, saved):
    count = gathered.shape[0]
    half = EXPERTS * saved[0].shape[1] // 2
    info_at = 2 * width // INFO
    whole = pl.BlockSpec((count, half), lambda k: (0, 0))
    return pl.pallas_call(
        slopes_kernel,
        grid=(1,),
        in_specs=[
            pl.BlockSpec(memory_space=pltpu.SMEM),
            pl.BlockSpec((count, INFO), lambda k: (0, info_at)),
        ]
        + [pl.BlockSpec(saved[0].shape, lambda k: (0, 0))] * EXPERTS,
        out_specs=[whole, whole],
        out_shape=[jax.ShapeDtypeStruct((count, half), jnp.float32)] * 2,
        compiler_params=pltpu.CompilerParams(vmem_limit_bytes=VMEM),
        cost_estimate=pl.CostEstimate(
            flops=4 * count * half * saved[0].shape[0],
            bytes_accessed=3 << 20,
            transcendentals=count * half,
        ),
    )(e0, gathered, *saved)


def body(
    fwd_in, fwd_routes, router, bwd_in, bwd_routes, bwd_gates, w_gate, w_up, w_down, saved_pre
):
    width = fwd_in.shape[1]
    x = shift_and_swap(fwd_in, 1)
    q = shift_and_swap(bwd_in, -1)
    info = jnp.concatenate(
        [fwd_routes.astype(jnp.float32), slot_places(bwd_routes).astype(jnp.float32)]
        + three_terms(bwd_gates),
        axis=1,
    ).astype(jnp.bfloat16)
    info = swap(jnp.pad(info, ((0, 0), (0, INFO - info.shape[1]))))
    columns = swap(jnp.pad(router[0].T, ((0, 16 - EXPERTS), (0, 0))))
    after = lax.optimization_barrier
    x, q, info, columns, next_gate, next_up, next_down, kept_pre = after(
        (x, q, info, columns, w_gate[0], w_up[0], w_down[0], saved_pre[:, 0])
    )
    gathered = lax.all_gather(jnp.concatenate([x, q, info], axis=1), "y", axis=0, tiled=True)
    a0 = swap(next_gate)
    a0, next_up = after((a0, next_up))
    a1, a2, b0 = other_plane(a0), other_core(a0), swap(next_up)
    a1, b0, next_down = after((a1, b0, next_down))
    a3, b1, b2, c0 = other_core(a1), other_plane(b0), other_core(b0), swap(next_down)
    b1, c0, wg = after((b1, c0, jnp.concatenate([a0, a1, a2, a3], axis=1)))
    b3, c1, c2 = other_core(b1), other_plane(c0), other_core(c0)

    gathered = after((gathered, c0))[0]
    wu = jnp.concatenate([b0, b1, b2, b3], axis=1)
    rows = gathered[:, :width]
    grads = gathered[:, width : 2 * width]
    facts = gathered[:, 2 * width :].astype(jnp.float32)
    froutes = facts[:, 0:2].astype(jnp.int32)
    e0 = lax.axis_index("c") * 2 + lax.axis_index("v")
    lane = w_gate.shape[2]

    def per_block(routes, values):
        columns = []
        for number in range(EXPERTS):
            picked = jnp.where(routes == (e0 ^ number), values, jnp.zeros((), values.dtype))
            columns.append(jnp.sum(picked, axis=1, keepdims=True))
        return columns

    def side_by_side(columns):
        shape = (columns[0].shape[0], lane)
        return jnp.concatenate([jnp.broadcast_to(column, shape) for column in columns], axis=1)

    score = jax.nn.sigmoid(
        lax.dot_general(rows, columns, (((1,), (1,)), ((), ())), preferred_element_type=jnp.float32)
    )
    chosen = jnp.concatenate(
        [
            jnp.sum(
                jnp.where(froutes[:, k : k + 1] == jnp.arange(16)[None, :], score, 0.0),
                axis=1,
                keepdims=True,
            )
            for k in range(TOP)
        ],
        axis=1,
    )
    fgates = chosen / jnp.sum(chosen, axis=1, keepdims=True)
    fweight = side_by_side(per_block(froutes, fgates))
    gpre = jnp.dot(rows, wg, preferred_element_type=jnp.float32)
    upre = jnp.dot(rows, wu, preferred_element_type=jnp.float32)
    hidden = (jax.nn.silu(gpre) * upre * fweight).astype(jnp.bfloat16)

    c1, hidden = after((c1, hidden))
    c3 = other_core(c1)
    kept_pre = after((kept_pre, c3))[0]
    saved = [saved_of_lane(kept_pre, number) for number in range(EXPERTS)]
    wd = jnp.concatenate([c0, c1, c2, c3], axis=0)
    fpart = jnp.dot(hidden, wd, preferred_element_type=jnp.float32)
    slope_gate, slope_up = slopes(
        e0.astype(jnp.int32).reshape(1), after((gathered, hidden))[0], width, saved
    )
    dhid = lax.dot_general(
        gathered[:, width : 2 * width], wd, (((1,), (1,)), ((), ())), preferred_element_type=jnp.float32
    )
    dgate = (dhid * slope_gate).astype(jnp.bfloat16)
    dup = (dhid * slope_up).astype(jnp.bfloat16)
    ring = [Chain(fpart, 1, 4), Chain(fpart, -1, 3)]
    firsts = [chain.total.astype(jnp.bfloat16) for chain in ring]
    dgate, dup = after((dgate, dup, *firsts))[:2]
    bpart = lax.dot_general(
        dgate, wg, (((1,), (1,)), ((), ())), preferred_element_type=jnp.float32
    ) + lax.dot_general(dup, wu, (((1,), (1,)), ((), ())), preferred_element_type=jnp.float32)
    ring += [Chain(bpart, 1, 3), Chain(bpart, -1, 4)]
    for _ in range(4):
        for chain in ring:
            chain.step()
    fsum = own_block(fpart, 0) + ring[0].total + ring[1].total
    bsum = own_block(bpart, 0) + ring[2].total + ring[3].total
    fwd_out = (x.astype(jnp.float32) + fsum).astype(jnp.bfloat16)
    bwd_out = (q.astype(jnp.float32) + bsum).astype(jnp.bfloat16)
    return (swap(fwd_out), swap(bwd_out))


def solution(mesh):
    fine = Mesh(mesh.devices.reshape(SIZES), AXES)
    section = ("x", "h", "c")
    part = ("u", "v", "y")
    both = P(AXES, None)
    in_specs = (
        both,
        both,
        P(section, None, None),
        both,
        both,
        both,
        P(section, None, part),
        P(section, None, part),
        P(section, part, None),
        P(None, section, None, part),
    )
    return jax.shard_map(
        body, mesh=fine, in_specs=in_specs, out_specs=(both, both), check_vma=False
    )
```

```python
import jax
import jax.numpy as jnp
from jax import lax
from jax.experimental import pallas as pl
from jax.experimental.pallas import tpu as pltpu
from jax.sharding import Mesh, PartitionSpec as P

EXPERTS = 4
TOP = 2
CAP = 34
LANES = 8
INFO = 128
VMEM = 32 << 20

AXES = ("x", "h", "c", "u", "v", "y")
SIZES = (4, 2, 2, 2, 2, 8)


def swap(array):
    return lax.ppermute(array, ("c", "u"), [(0, 0), (1, 2), (2, 1), (3, 3)])


def shift_and_swap(array, by):
    pairs = []
    for p in range(16):
        q = (p + by) % 16
        for u in range(2):
            source = p * 2 + u
            target = (q // 2) * 4 + u * 2 + q % 2
            pairs.append((source, target))
    return lax.ppermute(array, ("x", "h", "c", "u"), pairs)


def other_plane(array):
    return lax.ppermute(array, "v", [(0, 1), (1, 0)])


def other_core(array):
    return lax.ppermute(array, "c", [(0, 1), (1, 0)])


def saved_of_lane(saved, number):
    rows = saved.shape[1] // EXPERTS
    expert = lax.axis_index("u") * 2 + lax.axis_index("v")
    part = lax.dynamic_slice_in_dim(saved, (expert ^ number) * rows, rows, axis=1)
    pairs = []
    for c in range(2):
        for e in range(4):
            z = e ^ number
            pairs.append((c * 4 + e, (z // 2) * 4 + c * 2 + z % 2))
    return lax.ppermute(jnp.concatenate([part[0], part[1]], axis=1), ("c", "u", "v"), pairs)


def slot_places(routes):
    rows = routes.shape[0]
    onehot = (routes[:, :, None] == jnp.arange(EXPERTS, dtype=jnp.int32)[None, None, :]).astype(
        jnp.int32
    )
    onehot = onehot.reshape(rows * TOP, EXPERTS)
    before = jnp.cumsum(onehot, axis=0) - onehot
    slot = jnp.sum(before * onehot, axis=1).reshape(rows, TOP)
    return routes * CAP + slot


def three_terms(values):
    high = lax.reduce_precision(values, 8, 7)
    middle = lax.reduce_precision(values - high, 8, 7)
    low = values - high - middle
    return [high, middle, low]


def neighbour(array, by):
    return lax.ppermute(array, "y", [(i, (i + by) % LANES) for i in range(LANES)])


def own_block(terms, distance):
    rows = terms.shape[0] // LANES
    place = (lax.axis_index("y") + distance) % LANES
    return lax.dynamic_slice_in_dim(terms, place * rows, rows, axis=0)


class Chain:
    def __init__(self, terms, by, length):
        self.terms, self.by, self.left = terms, by, length
        self.total = own_block(terms, by * length)

    def step(self):
        if self.left:
            self.left -= 1
            received = neighbour(self.total.astype(jnp.bfloat16), self.by).astype(jnp.float32)
            self.total = received
            if self.left:
                self.total = received + own_block(self.terms, self.by * self.left)


def slopes_kernel(e0_ref, info_ref, *refs):
    saved_refs = refs[0:4]
    slope_gate_ref, slope_up_ref = refs[4:]
    count = info_ref.shape[0]
    slots, lane = saved_refs[0].shape[0], saved_refs[0].shape[1] // 2
    facts = info_ref[...].astype(jnp.float32)
    places = [facts[:, 2:3], facts[:, 3:4]]
    gates = [
        facts[:, 4 + k : 5 + k] + facts[:, 6 + k : 7 + k] + facts[:, 8 + k : 9 + k]
        for k in range(TOP)
    ]
    source = lax.broadcasted_iota(jnp.int32, (count, 1), 0) // (count // LANES)
    start = (source * CAP + 1).astype(jnp.float32)
    spot = (lax.broadcasted_iota(jnp.int32, (1, slots), 1) + 1).astype(jnp.float32)
    for block in range(EXPERTS):
        low = ((e0_ref[0] ^ block) * CAP).astype(jnp.float32)
        weight = jnp.zeros((count, 1), jnp.float32)
        target = jnp.zeros((count, 1), jnp.float32)
        for k in range(TOP):
            named = jnp.logical_and(places[k] >= low, places[k] < low + CAP)
            weight = weight + jnp.where(named, gates[k], 0.0)
            target = target + jnp.where(named, start + places[k] - low, 0.0)
        pick = jnp.where(target == spot, 1.0, 0.0).astype(jnp.bfloat16)
        kept = jnp.dot(pick, saved_refs[block][...], preferred_element_type=jnp.float32)
        apre, bpre = kept[:, :lane], kept[:, lane:]
        sig = jax.nn.sigmoid(apre)
        columns = slice(block * lane, (block + 1) * lane)
        slope_gate_ref[:, columns] = bpre * sig * (1.0 + apre * (1.0 - sig)) * weight
        slope_up_ref[:, columns] = apre * sig * weight


def slopes(e0, gathered, width, saved):
    count = gathered.shape[0]
    half = EXPERTS * saved[0].shape[1] // 2
    info_at = 2 * width // INFO
    whole = pl.BlockSpec((count, half), lambda k: (0, 0))
    return pl.pallas_call(
        slopes_kernel,
        grid=(1,),
        in_specs=[
            pl.BlockSpec(memory_space=pltpu.SMEM),
            pl.BlockSpec((count, INFO), lambda k: (0, info_at)),
        ]
        + [pl.BlockSpec(saved[0].shape, lambda k: (0, 0))] * EXPERTS,
        out_specs=[whole, whole],
        out_shape=[jax.ShapeDtypeStruct((count, half), jnp.float32)] * 2,
        compiler_params=pltpu.CompilerParams(vmem_limit_bytes=VMEM),
        cost_estimate=pl.CostEstimate(
            flops=4 * count * half * saved[0].shape[0],
            bytes_accessed=3 << 20,
            transcendentals=count * half,
        ),
    )(e0, gathered, *saved)


def body(
    fwd_in, fwd_routes, router, bwd_in, bwd_routes, bwd_gates, w_gate, w_up, w_down, saved_pre
):
    width = fwd_in.shape[1]
    x = shift_and_swap(fwd_in, 1)
    q = shift_and_swap(bwd_in, -1)
    info = jnp.concatenate(
        [fwd_routes.astype(jnp.float32), slot_places(bwd_routes).astype(jnp.float32)]
        + three_terms(bwd_gates),
        axis=1,
    ).astype(jnp.bfloat16)
    info = swap(jnp.pad(info, ((0, 0), (0, INFO - info.shape[1]))))
    columns = swap(jnp.pad(router[0].T, ((0, 16 - EXPERTS), (0, 0))))
    after = lax.optimization_barrier
    a0 = swap(w_gate[0])
    x, q, info, columns, a0, next_up, next_down, kept_pre = after(
        (x, q, info, columns, a0, w_up[0], w_down[0], saved_pre[:, 0])
    )
    gathered = lax.all_gather(jnp.concatenate([x, q, info], axis=1), "y", axis=0, tiled=True)
    a1, a2, b0 = other_plane(a0), other_core(a0), swap(next_up)
    a1, b0, next_down = after((a1, b0, next_down))
    a3, b1, b2, c0 = other_core(a1), other_plane(b0), other_core(b0), swap(next_down)
    b1, c0, wg, kept_pre = after(
        (b1, c0, jnp.concatenate([a0, a1, a2, a3], axis=1), kept_pre)
    )
    b3, c1, c2 = other_core(b1), other_plane(c0), other_core(c0)
    saved = [saved_of_lane(kept_pre, number) for number in range(EXPERTS)]

    gathered = after((gathered, c0))[0]
    wu = jnp.concatenate([b0, b1, b2, b3], axis=1)
    rows = gathered[:, :width]
    grads = gathered[:, width : 2 * width]
    facts = gathered[:, 2 * width :].astype(jnp.float32)
    froutes = facts[:, 0:2].astype(jnp.int32)
    e0 = lax.axis_index("c") * 2 + lax.axis_index("v")
    lane = w_gate.shape[2]

    def per_block(routes, values):
        columns = []
        for number in range(EXPERTS):
            picked = jnp.where(routes == (e0 ^ number), values, jnp.zeros((), values.dtype))
            columns.append(jnp.sum(picked, axis=1, keepdims=True))
        return columns

    def side_by_side(columns):
        shape = (columns[0].shape[0], lane)
        return jnp.concatenate([jnp.broadcast_to(column, shape) for column in columns], axis=1)

    score = jax.nn.sigmoid(
        lax.dot_general(rows, columns, (((1,), (1,)), ((), ())), preferred_element_type=jnp.float32)
    )
    chosen = jnp.concatenate(
        [
            jnp.sum(
                jnp.where(froutes[:, k : k + 1] == jnp.arange(16)[None, :], score, 0.0),
                axis=1,
                keepdims=True,
            )
            for k in range(TOP)
        ],
        axis=1,
    )
    fgates = chosen / jnp.sum(chosen, axis=1, keepdims=True)
    fweight = side_by_side(per_block(froutes, fgates))
    gpre = jnp.dot(rows, wg, preferred_element_type=jnp.float32)
    c1, gpre = after((c1, gpre))
    upre = jnp.dot(rows, wu, preferred_element_type=jnp.float32)
    hidden = (jax.nn.silu(gpre) * upre * fweight).astype(jnp.bfloat16)

    c3 = other_core(c1)
    wd = jnp.concatenate([c0, c1, c2, c3], axis=0)
    fpart = jnp.dot(hidden, wd, preferred_element_type=jnp.float32)
    slope_gate, slope_up = slopes(
        e0.astype(jnp.int32).reshape(1), after((gathered, hidden))[0], width, saved
    )
    dhid = lax.dot_general(
        gathered[:, width : 2 * width], wd, (((1,), (1,)), ((), ())), preferred_element_type=jnp.float32
    )
    dgate = (dhid * slope_gate).astype(jnp.bfloat16)
    dup = (dhid * slope_up).astype(jnp.bfloat16)
    ring = [Chain(fpart, 1, 4), Chain(fpart, -1, 3)]
    firsts = [chain.total.astype(jnp.bfloat16) for chain in ring]
    dgate, dup = after((dgate, dup, *firsts))[:2]
    bpart = lax.dot_general(
        dgate, wg, (((1,), (1,)), ((), ())), preferred_element_type=jnp.float32
    ) + lax.dot_general(dup, wu, (((1,), (1,)), ((), ())), preferred_element_type=jnp.float32)
    ring += [Chain(bpart, 1, 3), Chain(bpart, -1, 4)]
    for _ in range(4):
        for chain in ring:
            chain.step()
        for pair in (ring[:2], ring[2:]):
            pair[0].total, pair[1].total = after((pair[0].total, pair[1].total))
    fsum = own_block(fpart, 0) + ring[0].total + ring[1].total
    bsum = own_block(bpart, 0) + ring[2].total + ring[3].total
    fwd_out = (x.astype(jnp.float32) + fsum).astype(jnp.bfloat16)
    bwd_out = (q.astype(jnp.float32) + bsum).astype(jnp.bfloat16)
    return (swap(fwd_out), swap(bwd_out))


def solution(mesh):
    fine = Mesh(mesh.devices.reshape(SIZES), AXES)
    section = ("x", "h", "c")
    part = ("u", "v", "y")
    both = P(AXES, None)
    in_specs = (
        both,
        both,
        P(section, None, None),
        both,
        both,
        both,
        P(section, None, part),
        P(section, None, part),
        P(section, part, None),
        P(None, section, None, part),
    )
    return jax.shard_map(
        body, mesh=fine, in_specs=in_specs, out_specs=(both, both), check_vma=False
    )
```
